256 devices in a mesh: row: 8 (over x, y_lo), col: 32 (over y_hi, z, core).
Axes of the slice: x: 4, y: 4 (y_hi: 2, y_lo: 2; y = y_hi * 2 + y_lo), z: 8, core: 2. Of those that a mesh axis runs over, the one named last changes fastest.
Arguments:
- amplitudes: bfloat16 [4096, 65536], P('row', 'col'), may hold values from -6 to 6, as said below
- integrals: bfloat16 [65536, 6144], P('col', 'row'), may hold values from -0.0234375 to 0.0234375
- cd_irreps: int32 [512], P('col'), may hold values from 0 to 7
- ab_irreps: int32 [48], P('row'), may hold values from 0 to 7
- slab_amplitudes: bfloat16 [4096, 6144], P('col', 'row'), may hold values from -6 to 6, as said below
- occ_fock: float32 [64, 64], replicated, may hold values from -0.75 to 0.75
Outputs:
- update: float32 [4096, 6144], P('col', 'row')
The draws below stay inside these ranges and needn't reach their ends.
Inputs may be any that keep to these rules, and one draw needn't show every extreme that they name: Antisymmetric in the occupied pair: amplitudes[i * 64 + j, c] = -amplitudes[j * 64 + i, c] exactly. Antisymmetric in the occupied pair: slab_amplitudes[i * 64 + j, b] = -slab_amplitudes[j * 64 + i, b] exactly.
All inputs are finite; a program needn't handle non-finite values.
Results may differ from the reference program's by a relative error of at most 0.0003.
Values may be sent and summed in bfloat16 or wider, within the bound.
No kernel may reach another device: no remote copies, remote signals or barrier semaphores. Data moves between devices by JAX's collectives and lax.ppermute only.
A program may use at most 192 MiB of HBM per device.

```python
import math
import jax
import jax.numpy as jnp
import numpy as np
from jax import lax

NO = 64
TILE = 128
IRREPS = 8
CD = 65536
AB = 6144


def mirror_pairs(sample, columns):
    return ((sample - jnp.swapaxes(sample, 0, 1)) * 0.7071).reshape(NO * NO, columns).astype(jnp.bfloat16)


def draw_amplitudes(key, part):
    key = jax.random.fold_in(key, 11)
    sample = jnp.clip(jax.random.normal(key, (NO, NO, CD), jnp.float32), -4.0, 4.0)
    return mirror_pairs(sample, CD)


def draw_slab_amplitudes(key, part):
    key = jax.random.fold_in(key, 23)
    sample = jnp.clip(jax.random.normal(key, (NO, NO, AB), jnp.float32), -4.0, 4.0)
    return mirror_pairs(sample, AB)


def place_ends(drawn, rng, smallest, largest):
    shape = drawn.shape
    place = [jax.random.randint(jax.random.fold_in(rng, axis), (), 0, shape[axis]) for axis in range(len(shape))]
    drawn = drawn.at[tuple(place)].set(smallest)
    longest = shape.index(max(shape))
    place[longest] = (place[longest] + 1) % shape[longest]
    return drawn.at[tuple(place)].set(largest)


def level_of(stream_key, extent, split, low, largest):
    factor_of, own = 1.0, jax.random.fold_in(stream_key, 6)
    for dim, shards_of in split:
        heights = jnp.exp(jax.random.uniform(jax.random.fold_in(own, dim), (shards_of,), jnp.float32, low / len(split), largest / len(split)))
        factor_of = factor_of * jnp.repeat(heights, extent[dim] // shards_of).reshape([-1 if axis == dim else 1 for axis in range(len(extent))])
    return factor_of


def rank_bounds(count, slope):
    weights = [(1 << 20) // math.isqrt(rank ** slope) + 1 for rank in range(1, count + 1)]
    scale = 1 + sum(weights) // (1 << 30)
    return np.cumsum(np.array([max(1, weight // scale) for weight in weights]))


def skewed_ids(rng, shape, amount, slope):
    listing = rank_bounds(amount, slope)
    pick = jax.random.randint(jax.random.fold_in(rng, 1), shape, 0, int(listing[amount - 1]))
    grade = jnp.searchsorted(jnp.asarray(listing, jnp.int32), pick, side="right")
    return jax.random.permutation(jax.random.fold_in(rng, 2), amount)[grade].astype(jnp.int32)


def gaussian(own_key, dims, deviation, limit, split=(), kind=jnp.bfloat16):
    result = deviation * jax.random.normal(own_key, dims, jnp.float32)
    if split:
        result = result * level_of(own_key, dims, split, -0.22, 0.18)
    return jnp.clip(result, -limit, limit).astype(kind)


def setup_inputs(seed: int = 0) -> dict:
    splits = jax.random.split(jax.random.key(seed), 7)
    return {
        "amplitudes": draw_amplitudes(jax.random.fold_in(splits[6], 71), 0),
        "integrals": gaussian(splits[1], (CD, AB), CD ** -0.5, 0.0234375, ((0, 32), (1, 8))),
        "cd_irreps": place_ends(skewed_ids(splits[2], (CD // TILE,), IRREPS, 2), jax.random.fold_in(splits[2], 3), 0, IRREPS - 1).astype(jnp.int32),
        "ab_irreps": place_ends(skewed_ids(splits[3], (AB // TILE,), IRREPS, 2), jax.random.fold_in(splits[3], 3), 0, IRREPS - 1).astype(jnp.int32),
        "slab_amplitudes": draw_slab_amplitudes(jax.random.fold_in(splits[6], 71), 0),
        "occ_fock": gaussian(splits[5], (NO, NO), NO ** -0.5, 0.75, (), jnp.float32),
    }


def reference(amplitudes, integrals, cd_irreps, ab_irreps, slab_amplitudes, occ_fock):
    matching = (cd_irreps[:, None] == ab_irreps[None, :]).astype(jnp.bfloat16)
    tiled_view = integrals.reshape(CD // TILE, TILE, AB // TILE, TILE) * matching[:, None, :, None]
    masked = tiled_view.reshape(CD, AB)
    ladder = jnp.dot(amplitudes, masked, preferred_element_type=jnp.float32)
    slab_wide = slab_amplitudes.astype(jnp.float32).reshape(NO, NO, AB)
    fock_term = jnp.einsum("ilb,lj->ijb", slab_wide, occ_fock.astype(jnp.float32), precision=lax.Precision.HIGHEST)
    combined = ladder.reshape(NO, NO, AB) + fock_term
    update = combined - jnp.swapaxes(combined, 0, 1)
    return update.reshape(NO * NO, AB)
```

```python
import jax
import jax.numpy as jnp
from jax import lax
from jax.sharding import PartitionSpec as P

X, LO, HI, Z, CORES = 4, 2, 2, 8, 2
SCALE = 64.0


def x_shift(step):
    return [(2 * x + l, 2 * ((x + step) % X) + l) for x in range(X) for l in range(LO)]


Y_SWAP = [(r, r ^ 1) for r in range(X * LO)]
CORE_SWAP = [(c, c ^ 1) for c in range(HI * Z * CORES)]
H_SWAP = [(c, c ^ 16) for c in range(HI * Z * CORES)]


def z_shift(step):
    return [
        (16 * h + 2 * z + k, 16 * h + 2 * ((z + step) % Z) + k)
        for h in range(HI)
        for z in range(Z)
        for k in range(CORES)
    ]


def masked_tiles(integrals, cd_irreps, ab_irreps):
    row_tiles = cd_irreps.shape[0]
    col_tiles = ab_irreps.shape[0]
    tile_size = integrals.shape[0] // row_tiles
    matching = (cd_irreps[:, None] == ab_irreps[None, :]).astype(jnp.bfloat16)
    tiled_view = (
        integrals.reshape(row_tiles, tile_size, col_tiles, tile_size) * matching[:, None, :, None]
    )
    return tiled_view.reshape(integrals.shape)


def own_pairs(amplitudes, x, l):
    depth = amplitudes.shape[1]
    t = amplitudes.reshape(8, 64, depth)
    following = lax.dynamic_slice(t, (0, 16 * ((x + 1) % 4), 0), (8, 16, depth))
    opposite = lax.dynamic_slice(t, (0, 16 * ((x + 2) % 4) + 8 * (l ^ (x // 2)), 0), (8, 8, depth))
    same = lax.dynamic_slice(t, (0, 16 * x, 0), (8, 16, depth))
    same = jnp.where(l == 1, jnp.concatenate([same[:, 8:], same[:, :8]], axis=1), same)
    same = jnp.stack([same[i, i + 1 : i + 9] for i in range(8)])
    return following, jnp.concatenate([opposite, same], axis=1)


def gather_chunk(own):
    half = own.shape[0] // 2
    partner = lax.ppermute(own, "row", Y_SWAP)
    left = lax.ppermute(own, "row", x_shift(1))
    right = lax.ppermute(own, "row", x_shift(-1))
    far_a = lax.ppermute(left[:half], "row", x_shift(1))
    far_b = lax.ppermute(right[half:], "row", x_shift(-1))
    left_partner = lax.ppermute(partner, "row", x_shift(1))
    right_partner = lax.ppermute(partner, "row", x_shift(-1))
    far = jnp.concatenate([far_a, far_b])
    far_partner = lax.ppermute(far, "row", Y_SWAP)
    return jnp.concatenate([own, partner, right, right_partner, far, far_partner, left, left_partner])


def reduce_chunk(partial, x, l, h, z, k):
    n = partial.shape[1]
    blocks = partial.reshape(4, 2, 2, 2, 16, n)
    mine = lax.dynamic_index_in_dim(blocks, k, 3, keepdims=False)
    theirs = lax.dynamic_index_in_dim(blocks, 1 - k, 3, keepdims=False)
    both = (mine + lax.ppermute(theirs, "col", CORE_SWAP)).reshape(2, 2, 2, 2, 16, n)

    def part_for(target):
        place = (0, (target // 4 - x) % 2, ((target // 2) % 2) ^ l, target % 2, 0, 0)
        return lax.dynamic_slice(both, place, (2, 1, 1, 1, 16, n)).reshape(2, 16, n)

    total = part_for(z)
    for step in (1, 7, 2, 6, 3, 5, 4):
        sent = (part_for((z + step) % 8) * SCALE).astype(jnp.float16)
        total = total + lax.ppermute(sent, "col", z_shift(step)).astype(jnp.float32) * (1 / SCALE)
    first_h = ((x + (z // 4 - x) % 2) % 4) // 2
    at = (first_h != h).astype(jnp.int32)
    kept = lax.dynamic_index_in_dim(total, at, 0, keepdims=False)
    other = lax.dynamic_index_in_dim(total, 1 - at, 0, keepdims=False)
    return kept + lax.ppermute(other, "col", H_SWAP)


def slot_weights(c, e):
    group, lo, i16 = c // 8, (c // 4) % 2, (2 * c + e) % 16
    t = lax.broadcasted_iota(jnp.int32, (64, 32), 1)
    j = lax.broadcasted_iota(jnp.int32, (64, 32), 0)
    slot = jnp.where(
        t < 16,
        16 * ((group + 1) % 4) + t,
        jnp.where(
            t < 24,
            16 * ((group + 2) % 4) + 8 * (lo ^ (group // 2)) + t - 16,
            16 * group + (i16 + t - 23) % 16,
        ),
    )
    return jnp.where(slot == j, jnp.where(t == 31, 1.0, 2.0), 0.0)


def per_device(amplitudes, integrals, cd_irreps, ab_irreps, slab_amplitudes, occ_fock):
    r, c = lax.axis_index("row"), lax.axis_index("col")
    x, l = r // 2, r % 2
    h, z, k = c // 16, (c // 2) % 8, c % 2
    panel = masked_tiles(integrals, cd_irreps, ab_irreps)
    depth, n = panel.shape
    following, others = own_pairs(amplitudes, x, l)
    summed = []
    for rows in (following, others):
        for e in range(2):
            own = rows[e::2].reshape(64, depth)
            partial = jnp.dot(gather_chunk(own), panel, preferred_element_type=jnp.float32)
            summed.append(reduce_chunk(partial, x, l, h, z, k))
    slab = slab_amplitudes.astype(jnp.float32).reshape(2, 64, n)
    combined = jnp.stack(
        [
            jnp.dot(
                jnp.concatenate([occ_fock.T, slot_weights(c, e)], axis=1),
                jnp.concatenate([slab[e], summed[e], summed[2 + e]]),
                precision=lax.Precision.HIGHEST,
            )
            for e in range(2)
        ]
    )
    received = lax.all_to_all(combined, "col", split_axis=1, concat_axis=0, tiled=True)
    update = combined - jnp.swapaxes(received, 0, 1)
    return update.reshape(128, n)


def solution(mesh):
    return jax.shard_map(
        per_device,
        mesh=mesh,
        in_specs=(P("row", "col"), P("col", "row"), P("col"), P("row"), P("col", "row"), P()),
        out_specs=P("col", "row"),
        check_vma=False,
    )
```

```python
import jax
import jax.numpy as jnp
from jax import lax
from jax.sharding import PartitionSpec as P

X, LO, HI, Z, CORES = 4, 2, 2, 8, 2
COLS = HI * Z * CORES
SCALE = 64.0


def x_shift(step):
    return [(2 * x + l, 2 * ((x + step) % X) + l) for x in range(X) for l in range(LO)]


Y_SWAP = [(r, r ^ 1) for r in range(X * LO)]
CORE_SWAP = [(c, c ^ 1) for c in range(COLS)]
H_SWAP = [(c, c ^ 16) for c in range(COLS)]
Z_GROUPS = [[16 * h + 2 * z + k for z in range(Z)] for h in range(HI) for k in range(CORES)]
HZ_GROUPS = [[2 * hz + k for hz in range(HI * Z)] for k in range(CORES)]


def partner_of(i, t):
    group, half, i16, i8 = i // 16, (i // 8) % 2, i % 16, i % 8
    following = 16 * ((group + 1) % 4) + (i16 + t) % 16
    opposite = 16 * ((group + 2) % 4) + 8 * (half ^ (group // 2)) + (i8 + t) % 8
    same = 16 * group + (i16 + t - 23) % 16
    return jnp.where(t < 16, following, jnp.where(t < 24, opposite, same))


def grid(rows, columns):
    return (
        lax.broadcasted_iota(jnp.int32, (rows, columns), 0),
        lax.broadcasted_iota(jnp.int32, (rows, columns), 1),
    )


def masked_tiles(integrals, cd_irreps, ab_irreps):
    row_tiles = cd_irreps.shape[0]
    col_tiles = ab_irreps.shape[0]
    tile_size = integrals.shape[0] // row_tiles
    matching = (cd_irreps[:, None] == ab_irreps[None, :]).astype(jnp.bfloat16)
    tiled_view = (
        integrals.reshape(row_tiles, tile_size, col_tiles, tile_size) * matching[:, None, :, None]
    )
    return tiled_view.reshape(integrals.shape)


def own_pairs(amplitudes, r):
    to, held = grid(256, 512)
    wanted = (to % 8) * 64 + partner_of(8 * r + to % 8, to // 8)
    pick = (wanted == held).astype(jnp.bfloat16)
    return jnp.dot(pick, amplitudes, preferred_element_type=jnp.float32).astype(jnp.bfloat16)


def core_sum(partial, k):
    n = partial.shape[1]
    blocks = partial.reshape(-1, HI * Z, CORES, 8, n)
    mine = lax.dynamic_index_in_dim(blocks, k, 2, keepdims=False)
    theirs = lax.dynamic_index_in_dim(blocks, 1 - k, 2, keepdims=False)
    return jnp.swapaxes(mine + lax.ppermute(theirs, "col", CORE_SWAP), 0, 1)


def per_device(amplitudes, integrals, cd_irreps, ab_irreps, slab_amplitudes, occ_fock):
    r, c = lax.axis_index("row"), lax.axis_index("col")
    x, l = r // 2, r % 2
    h, k = c // 16, c % 2
    n = integrals.shape[1]

    own = own_pairs(amplitudes, r)
    partner = lax.ppermute(own, "row", Y_SWAP)
    left = lax.ppermute(own, "row", x_shift(1))
    right = lax.ppermute(own, "row", x_shift(-1))

    slab, own = lax.optimization_barrier((slab_amplitudes, own))
    slab = slab.astype(jnp.float32).reshape(2, 64, n)
    fock = jnp.einsum("elb,lj->ejb", slab, occ_fock, precision=lax.Precision.HIGHEST)
    mirrored = lax.all_to_all(fock, "col", split_axis=1, concat_axis=0, tiled=True)
    fock_update = (fock - jnp.swapaxes(mirrored, 0, 1)).reshape(128, n)
    panel = masked_tiles(integrals, cd_irreps, ab_irreps)
    partner, left, right, fock_update = lax.optimization_barrier((partner, left, right, fock_update))

    from_left = lax.ppermute(jnp.concatenate([left[:128], partner[128:]]), "row", x_shift(1))
    from_right = lax.ppermute(jnp.concatenate([right[128:], partner[:128]]), "row", x_shift(-1))
    across = lax.ppermute(jnp.concatenate([left[:128], right[128:]]), "row", Y_SWAP)

    first = jnp.dot(
        jnp.concatenate([own, partner, left, right]), panel, preferred_element_type=jnp.float32
    )
    first = core_sum(first, k).reshape(HI, Z, -1, n).swapaxes(0, 1).reshape(-1, n)
    _, from_left, from_right, across = lax.optimization_barrier(
        (first, from_left, from_right, across)
    )
    left_partner = jnp.concatenate([across[:128], from_left[128:]])
    right_partner = jnp.concatenate([from_right[128:], across[128:]])
    far = jnp.concatenate([from_left[:128], from_right[:128]])
    first = lax.psum_scatter(
        first, "col", scatter_dimension=0, axis_index_groups=Z_GROUPS, tiled=True
    ).reshape(HI, -1, n)

    far_partner = jnp.concatenate(
        [
            lax.ppermute(left_partner[:96], "row", x_shift(1)),
            lax.ppermute(right_partner[96:192], "row", x_shift(-1)),
            lax.ppermute(far[192:], "row", Y_SWAP),
        ]
    )
    second = jnp.dot(
        jnp.concatenate([far, left_partner, right_partner, far_partner]),
        panel,
        preferred_element_type=jnp.float32,
    )
    second = (core_sum(second, k) * SCALE).astype(jnp.float16).reshape(HI * Z, -1, n)
    second = lax.all_to_all(
        second, "col", split_axis=0, concat_axis=0, axis_index_groups=HZ_GROUPS, tiled=True
    )
    second = second.astype(jnp.float32).sum(0) * (1 / SCALE)
    first, second = lax.optimization_barrier((first, second))

    kept = lax.dynamic_index_in_dim(first, h, 0, keepdims=False)
    other = lax.dynamic_index_in_dim(first, 1 - h, 0, keepdims=False)
    first = kept + lax.ppermute(other, "col", H_SWAP)
    summed = jnp.concatenate([first, second])

    to, at = grid(128, 64)
    source = at // 8
    dx = jnp.array([0, 0, 3, 1, 2, 3, 1, 2])
    dl = jnp.array([0, 1, 0, 0, 0, 1, 1, 1])
    i = 16 * ((x + dx[source]) % 4) + 8 * (l ^ dl[source]) + at % 8
    wanted = 2 * (to // 4) + to % 2
    held = jnp.where(to % 4 < 2, i, partner_of(i, c))
    spread = (wanted == held).astype(jnp.float32)
    sent = jnp.dot(spread, summed, precision=lax.Precision.HIGHEST)
    got = lax.all_to_all(sent, "col", split_axis=0, concat_axis=0, tiled=True)

    ej, at = grid(128, 128)
    i, j = 2 * c + ej // 64, ej % 64
    t, mine = at // 4, at % 2 == ej // 64
    weight = jnp.where(t == 31, 1.0, 2.0)
    forward = jnp.where(mine & (at % 4 < 2) & (partner_of(i, t) == j), weight, 0.0)
    backward = jnp.where(mine & (at % 4 >= 2) & (partner_of(j, t) == i), weight, 0.0)
    return fock_update + jnp.dot(forward - backward, got, precision=lax.Precision.HIGHEST)


def solution(mesh):
    return jax.shard_map(
        per_device,
        mesh=mesh,
        in_specs=(P("row", "col"), P("col", "row"), P("col"), P("row"), P("col", "row"), P()),
        out_specs=P("col", "row"),
        check_vma=False,
    )
```

```python
import jax
import jax.numpy as jnp
from jax import lax
from jax.experimental import pallas as pl
from jax.experimental.pallas import tpu as pltpu
from jax.sharding import PartitionSpec as P

X, LO, HI, Z, CORES = 4, 2, 2, 8, 2
COLS = HI * Z * CORES
SCALE = 64.0


def x_shift(step):
    return [(2 * x + l, 2 * ((x + step) % X) + l) for x in range(X) for l in range(LO)]


Y_SWAP = [(r, r ^ 1) for r in range(X * LO)]
CORE_SWAP = [(c, c ^ 1) for c in range(COLS)]
HZ_GROUPS = [[2 * hz + k for hz in range(HI * Z)] for k in range(CORES)]


def partner_of(i, t):
    group, half, i16, i8 = i // 16, (i // 8) % 2, i % 16, i % 8
    following = 16 * ((group + 1) % 4) + (i16 + t) % 16
    opposite = 16 * ((group + 2) % 4) + 8 * (half ^ (group // 2)) + (i8 + t) % 8
    same = 16 * group + (i16 + t - 23) % 16
    return jnp.where(t < 16, following, jnp.where(t < 24, opposite, same))


def grid(rows, columns):
    return (
        lax.broadcasted_iota(jnp.int32, (rows, columns), 0),
        lax.broadcasted_iota(jnp.int32, (rows, columns), 1),
    )


def masked_tiles(integrals, cd_irreps, ab_irreps):
    row_tiles = cd_irreps.shape[0]
    col_tiles = ab_irreps.shape[0]
    tile_size = integrals.shape[0] // row_tiles
    matching = (cd_irreps[:, None] == ab_irreps[None, :]).astype(jnp.bfloat16)
    tiled_view = (
        integrals.reshape(row_tiles, tile_size, col_tiles, tile_size) * matching[:, None, :, None]
    )
    return tiled_view.reshape(integrals.shape)


def own_pairs(amplitudes, r):
    to, held = grid(256, 512)
    wanted = (to % 8) * 64 + partner_of(8 * r + to % 8, to // 8)
    pick = (wanted == held).astype(jnp.bfloat16)
    return jnp.dot(pick, amplitudes, preferred_element_type=jnp.float32).astype(jnp.bfloat16)


def slot_sums_kernel(k_ref, panel_ref, *refs):
    *sources, mine_ref, theirs_ref = refs
    columns = panel_ref.shape[1]
    for s, source in enumerate(sources):
        sums = jnp.dot(source[...], panel_ref[...], preferred_element_type=jnp.float32)
        sums = sums.reshape(HI * Z, CORES, 8, columns)
        first = k_ref[0] == 0
        mine_ref[:, 8 * s : 8 * s + 8, :] = jnp.where(first, sums[:, 0], sums[:, 1])
        theirs_ref[:, 8 * s : 8 * s + 8, :] = jnp.where(first, sums[:, 1], sums[:, 0])


def slot_sums(k, panel, sources):
    depth, n = panel.shape
    tile = min(n, 256)
    rows = 8 * len(sources)
    out = jax.ShapeDtypeStruct((HI * Z, rows, n), jnp.float32)
    return pl.pallas_call(
        slot_sums_kernel,
        grid=(n // tile,),
        in_specs=[
            pl.BlockSpec(memory_space=pltpu.SMEM),
            pl.BlockSpec((depth, tile), lambda j: (0, j)),
        ]
        + [pl.BlockSpec((256, depth), lambda j: (0, 0))] * len(sources),
        out_specs=[pl.BlockSpec((HI * Z, rows, tile), lambda j: (0, 0, j))] * 2,
        out_shape=[out, out],
        compiler_params=pltpu.CompilerParams(vmem_limit_bytes=40 * 2**20),
        cost_estimate=pl.CostEstimate(
            flops=2 * 32 * rows * depth * n,
            bytes_accessed=2 * depth * (n + 32 * rows) + 4 * 32 * rows * n,
            transcendentals=0,
        ),
    )(k.reshape(1), panel, *sources)


def core_sum(mine, theirs):
    return ((mine + lax.ppermute(theirs, "col", CORE_SWAP)) * SCALE).astype(jnp.float16)


def col_sum(parts):
    got = lax.all_to_all(
        parts, "col", split_axis=0, concat_axis=0, axis_index_groups=HZ_GROUPS, tiled=True
    )
    return got.astype(jnp.float32).sum(0) * (1 / SCALE)


def exact_dot(a, b):
    return jnp.dot(a, b, precision=lax.Precision.HIGHEST)


def fock_terms(c, slab, occ_fock):
    ej, el = grid(128, 128)
    own = jnp.where(ej // 64 == el // 64, jnp.tile(occ_fock.T, (2, 2)), 0.0)
    mixed = 64 * ((ej // 2) % 2) + 2 * (ej // 4) + ej % 2
    order = (mixed == el).astype(jnp.float32)
    got = lax.all_to_all(
        exact_dot(exact_dot(order, own), slab), "col", split_axis=0, concat_axis=0, tiled=True
    )
    mirror = (2 * (el // 4) + (el // 2) % 2 == ej % 64) & (el % 2 == ej // 64)
    return exact_dot(own, slab) - exact_dot(mirror.astype(jnp.float32), got)


def per_device(amplitudes, integrals, cd_irreps, ab_irreps, slab_amplitudes, occ_fock):
    r, c = lax.axis_index("row"), lax.axis_index("col")
    x, l = r // 2, r % 2
    h, k = c // 16, c % 2

    own = own_pairs(amplitudes, r)
    partner = lax.ppermute(own, "row", Y_SWAP)
    left = lax.ppermute(own, "row", x_shift(1))
    right = lax.ppermute(own, "row", x_shift(-1))
    slab, _ = lax.optimization_barrier((slab_amplitudes, own))
    fock_update = fock_terms(c, slab.astype(jnp.float32), occ_fock)
    panel = masked_tiles(integrals, cd_irreps, ab_irreps)

    to_right = jnp.concatenate([left[:128], partner[128:]])
    to_left = jnp.concatenate([partner[:128], right[128:]])
    to_partner = jnp.concatenate([left[:128], right[128:]])
    to_right, to_left, to_partner, own, partner, left, right = lax.optimization_barrier(
        (to_right, to_left, to_partner, own, partner, left, right)
    )
    from_left = lax.ppermute(to_right, "row", x_shift(1))
    from_right = lax.ppermute(to_left, "row", x_shift(-1))
    across = lax.ppermute(to_partner, "row", Y_SWAP)
    first = core_sum(*slot_sums(k, panel, [own, partner, left, right]))

    to_right, to_left = across[:96], across[160:]
    to_partner = jnp.concatenate([from_left[96:128], from_right[128:160]])
    to_right, to_left, to_partner, first = lax.optimization_barrier(
        (to_right, to_left, to_partner, first)
    )
    first = col_sum(first)
    far_partner = jnp.concatenate(
        [
            lax.ppermute(to_right, "row", x_shift(1)),
            lax.ppermute(to_partner, "row", Y_SWAP),
            lax.ppermute(to_left, "row", x_shift(-1)),
        ]
    )
    second = core_sum(*slot_sums(k, panel, [from_left, from_right, across]))
    third = core_sum(*slot_sums(k, panel, [far_partner]))
    summed = jnp.concatenate([first, col_sum(jnp.concatenate([second, third], axis=1))])

    to, at = grid(128, 64)
    source = at // 8
    dx = jnp.where(h == 0, jnp.array([0, 0, 3, 1, 2, 1, 3, 2]), jnp.array([0, 0, 3, 1, 3, 2, 1, 2]))
    dl = jnp.where(h == 0, jnp.array([0, 1, 0, 0, 0, 1, 1, 1]), jnp.array([0, 1, 0, 0, 1, 0, 1, 1]))
    i = 16 * ((x + dx[source]) % 4) + 8 * (l ^ dl[source]) + at % 8
    wanted = 2 * (to // 4) + to % 2
    held = jnp.where(to % 4 < 2, i, partner_of(i, c))
    spread = (wanted == held).astype(jnp.float32)
    got = lax.all_to_all(exact_dot(spread, summed), "col", split_axis=0, concat_axis=0, tiled=True)

    ej, at = grid(128, 128)
    i, j = 2 * c + ej // 64, ej % 64
    t, mine = at // 4, at % 2 == ej // 64
    weight = jnp.where(t == 31, 1.0, 2.0)
    forward = jnp.where(mine & (at % 4 < 2) & (partner_of(i, t) == j), weight, 0.0)
    backward = jnp.where(mine & (at % 4 >= 2) & (partner_of(j, t) == i), weight, 0.0)
    return fock_update + exact_dot(forward - backward, got)


def solution(mesh):
    return jax.shard_map(
        per_device,
        mesh=mesh,
        in_specs=(P("row", "col"), P("col", "row"), P("col"), P("row"), P("col", "row"), P()),
        out_specs=P("col", "row"),
        check_vma=False,
    )
```

```python
import functools

import jax
import jax.numpy as jnp
from jax import lax
from jax.experimental import pallas as pl
from jax.experimental.pallas import tpu as pltpu
from jax.sharding import PartitionSpec as P

X, LO, HI, Z, CORES = 4, 2, 2, 8, 2
COLS = HI * Z * CORES
SCALE = 64.0
LADDER_SCALE, FOCK_SCALE = 4.0, 128.0
COST = 40 * 10**9
SCALARS = pl.BlockSpec(memory_space=pltpu.SMEM)


def x_shift(step):
    return [(2 * x + l, 2 * ((x + step) % X) + l) for x in range(X) for l in range(LO)]


Y_SWAP = [(r, r ^ 1) for r in range(X * LO)]
CORE_SWAP = [(c, c ^ 1) for c in range(COLS)]
HZ_GROUPS = [[2 * hz + k for hz in range(HI * Z)] for k in range(CORES)]


def partner_of(i, t):
    group, half = i >> 4, (i >> 3) & 1
    following = (((group + 1) & 3) << 4) + ((i + t) & 15)
    opposite = (((group + 2) & 3) << 4) + ((half ^ (group >> 1)) << 3) + ((i + t) & 7)
    same = (group << 4) + ((i + t - 23) & 15)
    return jnp.where(t < 16, following, jnp.where(t < 24, opposite, same))


def grid(rows, columns):
    return (
        lax.broadcasted_iota(jnp.int32, (rows, columns), 0),
        lax.broadcasted_iota(jnp.int32, (rows, columns), 1),
    )


def masked_tiles_kernel(cd_ref, ab_ref, integrals_ref, out_ref):
    j = pl.program_id(0)
    row_tiles = cd_ref.shape[0]
    size = integrals_ref.shape[0] // row_tiles
    for b in range(integrals_ref.shape[1] // size):
        irrep = ab_ref[j * (integrals_ref.shape[1] // size) + b]
        for a in range(row_tiles):
            at = (slice(a * size, a * size + size), slice(b * size, b * size + size))
            matching = (cd_ref[a] == irrep).astype(jnp.float32).astype(jnp.bfloat16)
            out_ref[at] = integrals_ref[at] * matching


def masked_tiles(integrals, cd_irreps, ab_irreps):
    depth, n = integrals.shape
    tile = min(n, 256)
    block = pl.BlockSpec((depth, tile), lambda j: (0, j))
    return pl.pallas_call(
        masked_tiles_kernel,
        grid=(n // tile,),
        in_specs=[SCALARS, SCALARS, block],
        out_specs=block,
        out_shape=jax.ShapeDtypeStruct((depth, n), jnp.bfloat16),
        compiler_params=pltpu.CompilerParams(vmem_limit_bytes=16 * 2**20),
        cost_estimate=pl.CostEstimate(flops=0, bytes_accessed=4 * depth * n, transcendentals=0),
    )(cd_irreps, ab_irreps, integrals)


def own_pairs_kernel(r_ref, amplitudes_ref, own_ref, right_ref, mirrored_ref):
    r = r_ref[0]
    x, l = r >> 1, r & 1
    to, held = grid(448, 512)
    rho, j = to & 7, (r << 3) + (to & 7)
    t = to >> 3
    direct = (rho << 6) + partner_of(j, t)
    before = (((x + 3) & 3) << 4) + ((j - t) & 15)
    opposite = (x + 2) & 3
    across = (opposite << 4) + ((l ^ (opposite >> 1)) << 3) + ((j - t) & 7)
    wanted = jnp.where(to < 256, direct, (rho << 6) + jnp.where(to < 384, before, across))
    sign = jnp.where(to < 256, 1.0, -1.0)
    pick = jnp.where(wanted == held, sign, 0.0).astype(jnp.bfloat16)
    rows = jnp.dot(pick, amplitudes_ref[...], preferred_element_type=jnp.float32)
    rows = rows.astype(jnp.bfloat16)
    own_ref[...] = rows[:256]
    right_ref[...] = rows[128:384]
    mirrored_ref[...] = rows[256:]


def by_depth(kernel, scalars, arrays, out_rows, flops=0):
    depth = arrays[0].shape[1]
    tile = min(depth, 512)
    outs = [jax.ShapeDtypeStruct((rows, depth), jnp.bfloat16) for rows in out_rows]
    return pl.pallas_call(
        kernel,
        grid=(depth // tile,),
        in_specs=[SCALARS] * len(scalars)
        + [pl.BlockSpec((a.shape[0], tile), lambda j: (0, j)) for a in arrays],
        out_specs=[pl.BlockSpec((rows, tile), lambda j: (0, j)) for rows in out_rows],
        out_shape=outs,
        compiler_params=pltpu.CompilerParams(vmem_limit_bytes=32 * 2**20),
        cost_estimate=pl.CostEstimate(flops=flops, bytes_accessed=0, transcendentals=0),
    )(*scalars, *arrays)


def second_phase_kernel(partner_ref, left_ref, mirrored_ref, right_out, across_out, far_out):
    right_out[:128] = partner_ref[128:]
    right_out[128:] = left_ref[64:128]
    across_out[:192] = mirrored_ref[...]
    across_out[192:] = left_ref[128:]
    far_out[...] = partner_ref[192:]


OWN, MIRROR = 0, 1
SOURCES = (
    ((OWN, 0, 0),) * 3,
    ((OWN, 0, 1),) * 3,
    ((OWN, 1, 0),) * 3,
    ((MIRROR, 3, 0), (OWN, 3, 0), (OWN, 3, 0)),
    ((OWN, 1, 1),) * 3,
    ((MIRROR, 0, 0), (MIRROR, 0, 0), (OWN, 2, 0)),
    ((MIRROR, 0, 1), (MIRROR, 0, 1), (OWN, 2, 1)),
    ((MIRROR, 3, 1), (OWN, 3, 1), (OWN, 3, 1)),
)
FIRST = (((0, 0, 256),), ((1, 0, 256),), ((2, 0, 256),), ((3, 128, 256), (3, 0, 128)))
SECOND = (
    ((0, 0, 256),),
    ((1, 0, 192), (2, 128, 192)),
    ((3, 0, 192), (4, 0, 64)),
    ((3, 192, 320), (2, 0, 128)),
)


def slot_sums_kernel(layout, k_ref, panel_ref, *refs):
    *arrays, mine_ref, theirs_ref = refs
    columns = panel_ref.shape[1]
    for s, pieces in enumerate(layout):
        rows = [arrays[at][start:end, :] for at, start, end in pieces]
        rows = rows[0] if len(rows) == 1 else jnp.concatenate(rows)
        sums = jnp.dot(rows, panel_ref[...], preferred_element_type=jnp.float32)
        sums = sums.reshape(HI * Z, CORES, 8, columns)
        first = k_ref[0] == 0
        mine_ref[:, 8 * s : 8 * s + 8, :] = jnp.where(first, sums[:, 0], sums[:, 1])
        theirs_ref[:, 8 * s : 8 * s + 8, :] = jnp.where(first, sums[:, 1], sums[:, 0])


def slot_sums(k, panel, layout, arrays, flops):
    depth, n = panel.shape
    tile = min(n, 256)
    rows = 8 * len(layout)
    out = jax.ShapeDtypeStruct((HI * Z, rows, n), jnp.float32)
    return pl.pallas_call(
        functools.partial(slot_sums_kernel, layout),
        grid=(n // tile,),
        in_specs=[SCALARS, pl.BlockSpec((depth, tile), lambda j: (0, j))]
        + [pl.BlockSpec(a.shape, lambda j: (0, 0)) for a in arrays],
        out_specs=[pl.BlockSpec((HI * Z, rows, tile), lambda j: (0, 0, j))] * 2,
        out_shape=[out, out],
        compiler_params=pltpu.CompilerParams(vmem_limit_bytes=40 * 2**20),
        cost_estimate=pl.CostEstimate(flops=flops, bytes_accessed=0, transcendentals=0),
    )(k.reshape(1), panel, *arrays)


def core_sum(mine, theirs):
    return ((mine + lax.ppermute(theirs, "col", CORE_SWAP)) * SCALE).astype(jnp.float16)


def send_to_slots(parts):
    got = lax.all_to_all(
        parts, "col", split_axis=0, concat_axis=0, axis_index_groups=HZ_GROUPS, tiled=True
    )
    return got.astype(jnp.float32).sum(0)


def exact_dot(a, b):
    return jnp.dot(
        a, b, precision=lax.Precision.HIGHEST, preferred_element_type=jnp.float32
    )


def whole(kernel, scalars, arrays, rows, n):
    tile = n

    def block(shape):
        if shape[-1] != n:
            return pl.BlockSpec(shape, lambda j: (0,) * len(shape))
        return pl.BlockSpec(shape[:-1] + (tile,), lambda j: (0,) * (len(shape) - 1) + (j,))

    return pl.pallas_call(
        kernel,
        grid=(n // tile,),
        in_specs=[SCALARS] + [block(a.shape) for a in arrays],
        out_specs=block((rows, n)),
        out_shape=jax.ShapeDtypeStruct((rows, n), jnp.float32),
        compiler_params=pltpu.CompilerParams(vmem_limit_bytes=32 * 2**20),
        cost_estimate=pl.CostEstimate(
            flops=0, bytes_accessed=sum(a.size * a.dtype.itemsize for a in arrays), transcendentals=0
        ),
    )(scalars, *arrays)


def fock_matrix(fock_ref):
    ej, el = grid(128, 128)
    return jnp.where((ej >> 6) == (el >> 6), fock_ref[...], 0.0)


def fock_kernel(_, fock_ref, slab_ref, out_ref):
    out_ref[...] = exact_dot(fock_matrix(fock_ref), slab_ref[...].astype(jnp.float32))


def spread_kernel(at_ref, first_ref, second_ref, fock_ref, out_ref):
    x, l, c = at_ref[0], at_ref[1], at_ref[2]
    to, at = grid(256, 64)
    source, rho = at >> 3, at & 7
    i = jnp.zeros_like(at)
    for s, ranges in enumerate(SOURCES):
        options = []
        for (kind, dx, dl), narrow in zip(ranges, (False, True, True)):
            group, half = (x + dx) & 3, l ^ dl
            if kind == OWN:
                options.append((group << 4) + (half << 3) + rho)
            elif narrow:
                opposite = (group + 2) & 3
                options.append((opposite << 4) + ((half ^ (opposite >> 1)) << 3) + ((rho - c) & 7))
            else:
                options.append((((group + 3) & 3) << 4) + (((half << 3) + rho - c) & 15))
        chosen = jnp.where(c < 16, options[0], jnp.where(c < 24, options[1], options[2]))
        i = jnp.where(source == s, chosen, i)
    wanted = ((to >> 3) << 1) + (to & 1)
    held = jnp.where((to & 2) == 0, i, partner_of(i, c))
    spread = jnp.where((wanted == held) & ((to & 4) == 0), LADDER_SCALE / SCALE, 0.0)
    to, ej = grid(256, 128)
    order = ((((to >> 1) & 1) << 6) + ((to >> 3) << 1) + (to & 1) == ej) & ((to & 4) != 0)
    out_ref[...] = exact_dot(
        jnp.concatenate([spread, jnp.where(order, FOCK_SCALE, 0.0)], axis=1),
        jnp.concatenate([first_ref[...], second_ref[...], fock_ref[...]]),
    )


def update_kernel(at_ref, fock_ref, got_ref, out_ref):
    ej, at = grid(128, 256)
    e, j = ej >> 6, ej & 63
    i, t, mine = 2 * at_ref[2] + e, at >> 3, (at & 1) == e
    weight = jnp.where(t == 31, 1 / LADDER_SCALE, 2 / LADDER_SCALE)
    forward = jnp.where(mine & ((at & 6) == 0) & (partner_of(i, t) == j), weight, 0.0)
    backward = jnp.where(mine & ((at & 6) == 2) & (partner_of(j, t) == i), weight, 0.0)
    mirror = jnp.where(mine & ((at & 4) != 0) & ((t << 1) + ((at >> 1) & 1) == j), 1 / FOCK_SCALE, 0.0)
    out_ref[...] = fock_ref[...] + exact_dot(forward - backward - mirror, got_ref[...])


def exchange(rows):
    return lax.all_to_all(rows, "col", split_axis=0, concat_axis=0, tiled=True)


def per_device(amplitudes, integrals, cd_irreps, ab_irreps, slab, occ_fock):
    r, c = lax.axis_index("row"), lax.axis_index("col")
    k = c % 2
    place = jnp.stack([r // 2, r % 2, c])
    n = integrals.shape[1]
    fock_twice = jnp.tile(occ_fock.T, (2, 2))

    own, to_right, mirrored = by_depth(
        own_pairs_kernel, [r.reshape(1)], [amplitudes], (256, 256, 192)
    )
    partner = lax.ppermute(own, "row", Y_SWAP)
    right = lax.ppermute(own, "row", x_shift(-1))
    left = lax.ppermute(to_right, "row", x_shift(1))
    fock = whole(fock_kernel, place, [fock_twice, slab], 128, n)
    panel = masked_tiles(integrals, cd_irreps, ab_irreps)

    partner, left, right = lax.optimization_barrier((partner, left, right))
    to_right, to_partner, to_far = by_depth(
        second_phase_kernel, [], [partner, left, mirrored], (192, 320, 64)
    )
    to_right, to_partner, to_far, partner, left, right, panel = lax.optimization_barrier(
        (to_right, to_partner, to_far, partner, left, right, panel)
    )
    right_partner = lax.ppermute(partner, "row", x_shift(-1))
    from_left = lax.ppermute(to_right, "row", x_shift(1))
    across = lax.ppermute(to_partner, "row", Y_SWAP)
    far = lax.ppermute(to_far, "row", x_shift(2))

    first = core_sum(*slot_sums(k, panel, FIRST, [own, partner, right, left], COST))
    mine, theirs = slot_sums(
        k, panel, SECOND, [right_partner, mirrored, from_left, across, far], COST
    )
    second = core_sum(mine, theirs)
    summed = send_to_slots(jnp.concatenate([first, second], axis=1))
    first, second = summed[:32], summed[32:]

    sent = whole(spread_kernel, place, [first, second, fock], 256, n).astype(jnp.float16)
    got = exchange(sent).astype(jnp.float32)
    return whole(update_kernel, place, [fock, got], 128, n)


def solution(mesh):
    return jax.shard_map(
        per_device,
        mesh=mesh,
        in_specs=(P("row", "col"), P("col", "row"), P("col"), P("row"), P("col", "row"), P()),
        out_specs=P("col", "row"),
        check_vma=False,
    )
```

```python
import functools

import jax
import jax.numpy as jnp
from jax import lax
from jax.experimental import pallas as pl
from jax.experimental.pallas import tpu as pltpu
from jax.sharding import PartitionSpec as P

X, LO, HI, Z, CORES = 4, 2, 2, 8, 2
COLS = HI * Z * CORES
SCALE = 64.0
LADDER_SCALE, FOCK_SCALE = 4.0, 128.0
COST = 40 * 10**9
SCALARS = pl.BlockSpec(memory_space=pltpu.SMEM)


def x_shift(step):
    return [(2 * x + l, 2 * ((x + step) % X) + l) for x in range(X) for l in range(LO)]


Y_SWAP = [(r, r ^ 1) for r in range(X * LO)]
CORE_SWAP = [(c, c ^ 1) for c in range(COLS)]
H_SWAP = [(c, c ^ 16) for c in range(COLS)]
Z_GROUPS = [[16 * h + 2 * z + k for z in range(Z)] for h in range(HI) for k in range(CORES)]
HZ_GROUPS = [[2 * hz + k for hz in range(HI * Z)] for k in range(CORES)]


def partner_of(i, t):
    group, half = i >> 4, (i >> 3) & 1
    following = (((group + 1) & 3) << 4) + ((i + t) & 15)
    opposite = (((group + 2) & 3) << 4) + ((half ^ (group >> 1)) << 3) + ((i + t) & 7)
    same = (group << 4) + ((i + t - 23) & 15)
    return jnp.where(t < 16, following, jnp.where(t < 24, opposite, same))


def slot_of(c):
    return ((c & 1) << 4) + (c >> 1)


def grid(rows, columns):
    return (
        lax.broadcasted_iota(jnp.int32, (rows, columns), 0),
        lax.broadcasted_iota(jnp.int32, (rows, columns), 1),
    )


def masked_tiles_kernel(cd_ref, ab_ref, integrals_ref, out_ref):
    j = pl.program_id(0)
    row_tiles = cd_ref.shape[0]
    size = integrals_ref.shape[0] // row_tiles
    for b in range(integrals_ref.shape[1] // size):
        irrep = ab_ref[j * (integrals_ref.shape[1] // size) + b]
        for a in range(row_tiles):
            at = (slice(a * size, a * size + size), slice(b * size, b * size + size))
            matching = (cd_ref[a] == irrep).astype(jnp.float32).astype(jnp.bfloat16)
            out_ref[at] = integrals_ref[at] * matching


def masked_tiles(integrals, cd_irreps, ab_irreps):
    depth, n = integrals.shape
    tile = min(n, 256)
    block = pl.BlockSpec((depth, tile), lambda j: (0, j))
    return pl.pallas_call(
        masked_tiles_kernel,
        grid=(n // tile,),
        in_specs=[SCALARS, SCALARS, block],
        out_specs=block,
        out_shape=jax.ShapeDtypeStruct((depth, n), jnp.bfloat16),
        compiler_params=pltpu.CompilerParams(vmem_limit_bytes=16 * 2**20),
        cost_estimate=pl.CostEstimate(flops=0, bytes_accessed=4 * depth * n, transcendentals=0),
    )(cd_irreps, ab_irreps, integrals)


def own_pairs_kernel(r_ref, amplitudes_ref, own_ref, right_ref, mirrored_ref, pick_ref):
    @pl.when(pl.program_id(0) == 0)
    def _():
        r = r_ref[0]
        x, l = r >> 1, r & 1
        to, held = grid(448, 512)
        rho, j = to & 7, (r << 3) + (to & 7)
        t = to >> 3
        direct = (rho << 6) + partner_of(j, t)
        before = (((x + 3) & 3) << 4) + ((j - t) & 15)
        opposite = (x + 2) & 3
        across = (opposite << 4) + ((l ^ (opposite >> 1)) << 3) + ((j - t) & 7)
        wanted = jnp.where(to < 256, direct, (rho << 6) + jnp.where(to < 384, before, across))
        sign = jnp.where(to < 256, 1.0, -1.0)
        pick_ref[...] = jnp.where(wanted == held, sign, 0.0).astype(jnp.bfloat16)

    rows = jnp.dot(pick_ref[...], amplitudes_ref[...], preferred_element_type=jnp.float32)
    rows = rows.astype(jnp.bfloat16)
    own_ref[...] = rows[:256]
    right_ref[...] = rows[128:384]
    mirrored_ref[...] = rows[256:]


def by_depth(kernel, scalars, arrays, out_rows, flops=0, scratch=()):
    depth = arrays[0].shape[1]
    tile = min(depth, 512)
    outs = [jax.ShapeDtypeStruct((rows, depth), jnp.bfloat16) for rows in out_rows]
    return pl.pallas_call(
        kernel,
        grid=(depth // tile,),
        in_specs=[SCALARS] * len(scalars)
        + [pl.BlockSpec((a.shape[0], tile), lambda j: (0, j)) for a in arrays],
        out_specs=[pl.BlockSpec((rows, tile), lambda j: (0, j)) for rows in out_rows],
        out_shape=outs,
        scratch_shapes=scratch,
        compiler_params=pltpu.CompilerParams(vmem_limit_bytes=32 * 2**20),
        cost_estimate=pl.CostEstimate(flops=flops, bytes_accessed=0, transcendentals=0),
    )(*scalars, *arrays)


def second_phase_kernel(
    k_ref, own_ref, partner_ref, right_ref, left_ref, mirrored_ref, right_out, across_out, far_out, core_out
):
    right_out[:128] = partner_ref[128:]
    right_out[128:] = left_ref[64:128]
    across_out[:192] = mirrored_ref[...]
    across_out[192:] = left_ref[128:]
    far_out[...] = partner_ref[192:]
    core_out[...] = core_rows(1 - k_ref[0], own_ref, partner_ref, right_ref, left_ref)


def core_rows(k, own_ref, partner_ref, right_ref, left_ref):
    at, at_left = pl.multiple_of(128 * k, 128), pl.multiple_of(128 * (1 - k), 128)
    return jnp.concatenate(
        [ref[pl.ds(at, 128), :] for ref in (own_ref, partner_ref, right_ref)]
        + [left_ref[pl.ds(at_left, 128), :]]
    )


def first_sums_kernel(
    k_ref, panel_ref, other_panel_ref, own_ref, partner_ref, right_ref, left_ref, got_ref, out_ref
):
    rows = core_rows(k_ref[0], own_ref, partner_ref, right_ref, left_ref)
    sums = jnp.dot(rows, panel_ref[...], preferred_element_type=jnp.float32)
    sums += jnp.dot(got_ref[...], other_panel_ref[...], preferred_element_type=jnp.float32)
    for s in range(4):
        source = sums[128 * s : 128 * s + 128].reshape(HI, Z, 8, sums.shape[1])
        for h in range(HI):
            out_ref[:, 32 * h + 8 * s : 32 * h + 8 * s + 8, :] = source[h]


def first_sums(k, panel, other_panel, arrays):
    depth, n = panel.shape
    tile = min(n, 256)
    column = pl.BlockSpec((depth, tile), lambda j: (0, j))
    return pl.pallas_call(
        first_sums_kernel,
        grid=(n // tile,),
        in_specs=[SCALARS, column, column] + [pl.BlockSpec(a.shape, lambda j: (0, 0)) for a in arrays],
        out_specs=pl.BlockSpec((Z, HI * 32, tile), lambda j: (0, 0, j)),
        out_shape=jax.ShapeDtypeStruct((Z, HI * 32, n), jnp.float32),
        compiler_params=pltpu.CompilerParams(vmem_limit_bytes=48 * 2**20),
        cost_estimate=pl.CostEstimate(flops=COST, bytes_accessed=0, transcendentals=0),
    )(k.reshape(1), panel, other_panel, *arrays)


OWN, MIRROR = 0, 1
SOURCES = (
    ((OWN, 0, 0),) * 3,
    ((OWN, 0, 1),) * 3,
    ((OWN, 1, 0),) * 3,
    ((MIRROR, 3, 0), (OWN, 3, 0), (OWN, 3, 0)),
    ((OWN, 1, 1),) * 3,
    ((MIRROR, 0, 0), (MIRROR, 0, 0), (OWN, 2, 0)),
    ((MIRROR, 0, 1), (MIRROR, 0, 1), (OWN, 2, 1)),
    ((MIRROR, 3, 1), (OWN, 3, 1), (OWN, 3, 1)),
)
SECOND = (
    ((0, 0, 256),),
    ((1, 0, 192), (2, 128, 192)),
    ((3, 0, 192), (4, 0, 64)),
    ((3, 192, 320), (2, 0, 128)),
)


def slot_sums_kernel(layout, k_ref, panel_ref, *refs):
    *arrays, mine_ref, theirs_ref = refs
    columns = panel_ref.shape[1]
    for s, pieces in enumerate(layout):
        rows = [arrays[at][start:end, :] for at, start, end in pieces]
        rows = rows[0] if len(rows) == 1 else jnp.concatenate(rows)
        sums = jnp.dot(rows, panel_ref[...], preferred_element_type=jnp.float32)
        sums = sums.reshape(CORES, HI * Z, 8, columns)
        first = k_ref[0] == 0
        mine_ref[:, 8 * s : 8 * s + 8, :] = jnp.where(first, sums[0], sums[1])
        theirs_ref[:, 8 * s : 8 * s + 8, :] = jnp.where(first, sums[1], sums[0])


def slot_sums(k, panel, layout, arrays, flops):
    depth, n = panel.shape
    tile = min(n, 256)
    rows = 8 * len(layout)
    out = jax.ShapeDtypeStruct((HI * Z, rows, n), jnp.float32)
    return pl.pallas_call(
        functools.partial(slot_sums_kernel, layout),
        grid=(n // tile,),
        in_specs=[SCALARS, pl.BlockSpec((depth, tile), lambda j: (0, j))]
        + [pl.BlockSpec(a.shape, lambda j: (0, 0)) for a in arrays],
        out_specs=[pl.BlockSpec((HI * Z, rows, tile), lambda j: (0, 0, j))] * 2,
        out_shape=[out, out],
        compiler_params=pltpu.CompilerParams(vmem_limit_bytes=40 * 2**20),
        cost_estimate=pl.CostEstimate(flops=flops, bytes_accessed=0, transcendentals=0),
    )(k.reshape(1), panel, *arrays)


def core_sum(mine, theirs):
    return ((mine + lax.ppermute(theirs, "col", CORE_SWAP)) * SCALE).astype(jnp.float16)


def send_to_slots(parts):
    got = lax.all_to_all(
        parts, "col", split_axis=0, concat_axis=0, axis_index_groups=HZ_GROUPS, tiled=True
    )
    return got.astype(jnp.float32).sum(0)


def send_to_z(parts):
    got = lax.all_to_all(
        parts, "col", split_axis=0, concat_axis=0, axis_index_groups=Z_GROUPS, tiled=True
    )
    return got.astype(jnp.float32).sum(0).reshape(HI, -1, parts.shape[2])


def exact_dot(a, b):
    return jnp.dot(
        a, b, precision=lax.Precision.HIGHEST, preferred_element_type=jnp.float32
    )


def whole(kernel, scalars, arrays, rows, n):
    tile = n

    def block(shape):
        if shape[-1] != n:
            return pl.BlockSpec(shape, lambda j: (0,) * len(shape))
        return pl.BlockSpec(shape[:-1] + (tile,), lambda j: (0,) * (len(shape) - 1) + (j,))

    return pl.pallas_call(
        kernel,
        grid=(n // tile,),
        in_specs=[SCALARS] + [block(a.shape) for a in arrays],
        out_specs=block((rows, n)),
        out_shape=jax.ShapeDtypeStruct((rows, n), jnp.float32),
        compiler_params=pltpu.CompilerParams(vmem_limit_bytes=32 * 2**20),
        cost_estimate=pl.CostEstimate(
            flops=0, bytes_accessed=sum(a.size * a.dtype.itemsize for a in arrays), transcendentals=0
        ),
    )(scalars, *arrays)


def fock_matrix(fock_ref):
    ej, el = grid(128, 128)
    return jnp.where((ej >> 6) == (el >> 6), fock_ref[...], 0.0)


def fock_kernel(_, fock_ref, slab_ref, out_ref):
    out_ref[...] = exact_dot(fock_matrix(fock_ref), slab_ref[...].astype(jnp.float32))


def spread_kernel(at_ref, first_ref, second_ref, fock_ref, out_ref):
    x, l, c = at_ref[0], at_ref[1], slot_of(at_ref[2])
    to, at = grid(256, 64)
    source, rho = at >> 3, at & 7
    i = jnp.zeros_like(at)
    for s, ranges in enumerate(SOURCES):
        options = []
        for (kind, dx, dl), narrow in zip(ranges, (False, True, True)):
            group, half = (x + dx) & 3, l ^ dl
            if kind == OWN:
                options.append((group << 4) + (half << 3) + rho)
            elif narrow:
                opposite = (group + 2) & 3
                options.append((opposite << 4) + ((half ^ (opposite >> 1)) << 3) + ((rho - c) & 7))
            else:
                options.append((((group + 3) & 3) << 4) + (((half << 3) + rho - c) & 15))
        chosen = jnp.where(c < 16, options[0], jnp.where(c < 24, options[1], options[2]))
        i = jnp.where(source == s, chosen, i)
    wanted = ((to >> 3) << 1) + (to & 1)
    held = jnp.where((to & 2) == 0, i, partner_of(i, c))
    spread = jnp.where((wanted == held) & ((to & 4) == 0), LADDER_SCALE / SCALE, 0.0)
    to, ej = grid(256, 128)
    order = ((((to >> 1) & 1) << 6) + ((to >> 3) << 1) + (to & 1) == ej) & ((to & 4) != 0)
    out_ref[...] = exact_dot(
        jnp.concatenate([spread, jnp.where(order, FOCK_SCALE, 0.0)], axis=1),
        jnp.concatenate([first_ref[...], second_ref[...], fock_ref[...]]),
    )


def update_kernel(at_ref, fock_ref, got_ref, out_ref):
    ej, at = grid(128, 256)
    e, j = ej >> 6, ej & 63
    i, peer, mine = 2 * at_ref[2] + e, at >> 3, (at & 1) == e
    t = slot_of(peer)
    weight = jnp.where(t == 31, 1 / LADDER_SCALE, 2 / LADDER_SCALE)
    forward = jnp.where(mine & ((at & 6) == 0) & (partner_of(i, t) == j), weight, 0.0)
    backward = jnp.where(mine & ((at & 6) == 2) & (partner_of(j, t) == i), weight, 0.0)
    mirror = jnp.where(mine & ((at & 4) != 0) & ((peer << 1) + ((at >> 1) & 1) == j), 1 / FOCK_SCALE, 0.0)
    out_ref[...] = fock_ref[...] + exact_dot(forward - backward - mirror, got_ref[...])


def exchange(rows):
    return lax.all_to_all(rows, "col", split_axis=0, concat_axis=0, tiled=True)


def per_device(amplitudes, integrals, cd_irreps, ab_irreps, slab, occ_fock):
    r, c = lax.axis_index("row"), lax.axis_index("col")
    k = c % 2
    place = jnp.stack([r // 2, r % 2, c])
    n = integrals.shape[1]
    fock_twice = jnp.tile(occ_fock.T, (2, 2))

    own, to_right, mirrored = by_depth(
        own_pairs_kernel,
        [r.reshape(1)],
        [amplitudes],
        (256, 256, 192),
        scratch=[pltpu.VMEM((448, 512), jnp.bfloat16)],
    )
    partner = lax.ppermute(own, "row", Y_SWAP)
    right = lax.ppermute(own, "row", x_shift(-1))
    left = lax.ppermute(to_right, "row", x_shift(1))
    fock = whole(fock_kernel, place, [fock_twice, slab], 128, n)
    integrals, _ = lax.optimization_barrier((integrals, own))
    panel = masked_tiles(integrals, cd_irreps, ab_irreps)
    other_panel = lax.ppermute(panel, "col", CORE_SWAP)

    partner, left, right, panel = lax.optimization_barrier((partner, left, right, panel))
    to_right, to_partner, to_far, to_core = by_depth(
        second_phase_kernel,
        [k.reshape(1)],
        [own, partner, right, left, mirrored],
        (192, 320, 64, 512),
    )
    to_right, to_partner, to_far, to_core, partner, left, right, panel = lax.optimization_barrier(
        (to_right, to_partner, to_far, to_core, partner, left, right, panel)
    )
    from_core = lax.ppermute(to_core, "col", CORE_SWAP)
    right_partner = lax.ppermute(partner, "row", x_shift(-1))
    from_left = lax.ppermute(to_right, "row", x_shift(1))
    across = lax.ppermute(to_partner, "row", Y_SWAP)
    far = lax.ppermute(to_far, "row", x_shift(2))

    first = first_sums(k, panel, other_panel, [own, partner, right, left, from_core])
    first = send_to_z((first * SCALE).astype(jnp.float16))
    mine, theirs = slot_sums(
        k, panel, SECOND, [right_partner, mirrored, from_left, across, far], COST
    )
    theirs, first = lax.optimization_barrier((theirs, first))
    h = c // 16
    kept = lax.dynamic_index_in_dim(first, h, 0, keepdims=False)
    other = lax.dynamic_index_in_dim(first, 1 - h, 0, keepdims=False)
    first = kept + lax.ppermute(other, "col", H_SWAP)
    second = send_to_slots(core_sum(mine, theirs))

    sent = whole(spread_kernel, place, [first, second, fock], 256, n).astype(jnp.float16)
    got = exchange(sent).astype(jnp.float32)
    return whole(update_kernel, place, [fock, got], 128, n)


def solution(mesh):
    return jax.shard_map(
        per_device,
        mesh=mesh,
        in_specs=(P("row", "col"), P("col", "row"), P("col"), P("row"), P("col", "row"), P()),
        out_specs=P("col", "row"),
        check_vma=False,
    )
```

```python
import functools

import jax
import jax.numpy as jnp
from jax import lax
from jax.experimental import pallas as pl
from jax.experimental.pallas import tpu as pltpu
from jax.sharding import PartitionSpec as P

X, LO, HI, Z, CORES = 4, 2, 2, 8, 2
COLS = HI * Z * CORES
SCALE = 64.0
LADDER_SCALE, FOCK_SCALE = 4.0, 128.0
COST = 40 * 10**9
SCALARS = pl.BlockSpec(memory_space=pltpu.SMEM)


def x_shift(step):
    return [(2 * x + l, 2 * ((x + step) % X) + l) for x in range(X) for l in range(LO)]


Y_SWAP = [(r, r ^ 1) for r in range(X * LO)]
CORE_SWAP = [(c, c ^ 1) for c in range(COLS)]
H_SWAP = [(c, c ^ 16) for c in range(COLS)]
Z_GROUPS = [[16 * h + 2 * z + k for z in range(Z)] for h in range(HI) for k in range(CORES)]
HZ_GROUPS = [[2 * hz + k for hz in range(HI * Z)] for k in range(CORES)]


def partner_of(i, t):
    group, half = i >> 4, (i >> 3) & 1
    following = (((group + 1) & 3) << 4) + ((i + t) & 15)
    opposite = (((group + 2) & 3) << 4) + ((half ^ (group >> 1)) << 3) + ((i + t) & 7)
    same = (group << 4) + ((i + t - 23) & 15)
    return jnp.where(t < 16, following, jnp.where(t < 24, opposite, same))


def slot_of(c):
    return ((c & 1) << 4) + (c >> 1)


def grid(rows, columns):
    return (
        lax.broadcasted_iota(jnp.int32, (rows, columns), 0),
        lax.broadcasted_iota(jnp.int32, (rows, columns), 1),
    )


def masked_tiles_kernel(cd_ref, ab_ref, integrals_ref, out_ref):
    j = pl.program_id(0)
    row_tiles = cd_ref.shape[0]
    size = integrals_ref.shape[0] // row_tiles
    for b in range(integrals_ref.shape[1] // size):
        irrep = ab_ref[j * (integrals_ref.shape[1] // size) + b]
        for a in range(row_tiles):
            at = (slice(a * size, a * size + size), slice(b * size, b * size + size))
            matching = (cd_ref[a] == irrep).astype(jnp.float32).astype(jnp.bfloat16)
            out_ref[at] = integrals_ref[at] * matching


def masked_tiles(integrals, cd_irreps, ab_irreps):
    depth, n = integrals.shape
    tile = min(n, 256)
    block = pl.BlockSpec((depth, tile), lambda j: (0, j))
    return pl.pallas_call(
        masked_tiles_kernel,
        grid=(n // tile,),
        in_specs=[SCALARS, SCALARS, block],
        out_specs=block,
        out_shape=jax.ShapeDtypeStruct((depth, n), jnp.bfloat16),
        compiler_params=pltpu.CompilerParams(vmem_limit_bytes=16 * 2**20),
        cost_estimate=pl.CostEstimate(flops=0, bytes_accessed=4 * depth * n, transcendentals=0),
    )(cd_irreps, ab_irreps, integrals)


def own_pairs_kernel(r_ref, amplitudes_ref, own_ref, right_ref, mirrored_ref, pick_ref):
    @pl.when(pl.program_id(0) == 0)
    def _():
        r = r_ref[0]
        x, l = r >> 1, r & 1
        to, held = grid(448, 512)
        rho, j = to & 7, (r << 3) + (to & 7)
        t = to >> 3
        direct = (rho << 6) + partner_of(j, t)
        before = (((x + 3) & 3) << 4) + ((j - t) & 15)
        opposite = (x + 2) & 3
        across = (opposite << 4) + ((l ^ (opposite >> 1)) << 3) + ((j - t) & 7)
        wanted = jnp.where(to < 256, direct, (rho << 6) + jnp.where(to < 384, before, across))
        sign = jnp.where(to < 256, 1.0, -1.0)
        pick_ref[...] = jnp.where(wanted == held, sign, 0.0).astype(jnp.bfloat16)

    rows = jnp.dot(pick_ref[...], amplitudes_ref[...], preferred_element_type=jnp.float32)
    rows = rows.astype(jnp.bfloat16)
    own_ref[...] = rows[:256]
    right_ref[...] = rows[128:384]
    mirrored_ref[...] = rows[256:]


def by_depth(kernel, scalars, arrays, out_rows, flops=0, scratch=()):
    depth = arrays[0].shape[1]
    tile = min(depth, 512)
    outs = [jax.ShapeDtypeStruct((rows, depth), jnp.bfloat16) for rows in out_rows]
    return pl.pallas_call(
        kernel,
        grid=(depth // tile,),
        in_specs=[SCALARS] * len(scalars)
        + [pl.BlockSpec((a.shape[0], tile), lambda j: (0, j)) for a in arrays],
        out_specs=[pl.BlockSpec((rows, tile), lambda j: (0, j)) for rows in out_rows],
        out_shape=outs,
        scratch_shapes=scratch,
        compiler_params=pltpu.CompilerParams(vmem_limit_bytes=32 * 2**20),
        cost_estimate=pl.CostEstimate(flops=flops, bytes_accessed=0, transcendentals=0),
    )(*scalars, *arrays)


def second_phase_kernel(
    k_ref, own_ref, partner_ref, right_ref, left_ref, mirrored_ref, right_out, across_out, far_out, core_out
):
    right_out[:128] = partner_ref[128:]
    right_out[128:] = left_ref[64:128]
    across_out[:192] = mirrored_ref[...]
    across_out[192:] = left_ref[128:]
    far_out[...] = partner_ref[192:]
    core_out[...] = core_rows(1 - k_ref[0], own_ref, partner_ref, right_ref, left_ref)


def core_rows(k, own_ref, partner_ref, right_ref, left_ref):
    at, at_left = pl.multiple_of(128 * k, 128), pl.multiple_of(128 * (1 - k), 128)
    return jnp.concatenate(
        [ref[pl.ds(at, 128), :] for ref in (own_ref, partner_ref, right_ref)]
        + [left_ref[pl.ds(at_left, 128), :]]
    )


def first_sums_kernel(
    k_ref, panel_ref, other_panel_ref, own_ref, partner_ref, right_ref, left_ref, got_ref, out_ref
):
    rows = core_rows(k_ref[0], own_ref, partner_ref, right_ref, left_ref)
    sums = jnp.dot(rows, panel_ref[...], preferred_element_type=jnp.float32)
    sums += jnp.dot(got_ref[...], other_panel_ref[...], preferred_element_type=jnp.float32)
    for s in range(4):
        source = sums[128 * s : 128 * s + 128].reshape(HI, Z, 8, sums.shape[1])
        for h in range(HI):
            out_ref[:, 32 * h + 8 * s : 32 * h + 8 * s + 8, :] = source[h]


def first_sums(k, panel, other_panel, arrays):
    depth, n = panel.shape
    tile = min(n, 256)
    column = pl.BlockSpec((depth, tile), lambda j: (0, j))
    return pl.pallas_call(
        first_sums_kernel,
        grid=(n // tile,),
        in_specs=[SCALARS, column, column] + [pl.BlockSpec(a.shape, lambda j: (0, 0)) for a in arrays],
        out_specs=pl.BlockSpec((Z, HI * 32, tile), lambda j: (0, 0, j)),
        out_shape=jax.ShapeDtypeStruct((Z, HI * 32, n), jnp.float32),
        compiler_params=pltpu.CompilerParams(vmem_limit_bytes=48 * 2**20),
        cost_estimate=pl.CostEstimate(flops=COST, bytes_accessed=0, transcendentals=0),
    )(k.reshape(1), panel, other_panel, *arrays)


OWN, MIRROR = 0, 1
SOURCES = (
    ((OWN, 0, 0),) * 3,
    ((OWN, 0, 1),) * 3,
    ((OWN, 1, 0),) * 3,
    ((MIRROR, 3, 0), (OWN, 3, 0), (OWN, 3, 0)),
    ((OWN, 1, 1),) * 3,
    ((MIRROR, 0, 0), (MIRROR, 0, 0), (OWN, 2, 0)),
    ((MIRROR, 0, 1), (MIRROR, 0, 1), (OWN, 2, 1)),
    ((MIRROR, 3, 1), (OWN, 3, 1), (OWN, 3, 1)),
)
SECOND = (
    ((0, 0, 256),),
    ((1, 0, 192), (2, 128, 192)),
    ((3, 0, 192), (4, 0, 64)),
    ((3, 192, 320), (2, 0, 128)),
)


def slot_sums_kernel(layout, k_ref, panel_ref, *refs):
    *arrays, mine_ref, theirs_ref = refs
    columns = panel_ref.shape[1]
    for s, pieces in enumerate(layout):
        rows = [arrays[at][start:end, :] for at, start, end in pieces]
        rows = rows[0] if len(rows) == 1 else jnp.concatenate(rows)
        sums = jnp.dot(rows, panel_ref[...], preferred_element_type=jnp.float32)
        sums = sums.reshape(CORES, HI * Z, 8, columns)
        first = k_ref[0] == 0
        mine_ref[:, 8 * s : 8 * s + 8, :] = jnp.where(first, sums[0], sums[1])
        theirs_ref[:, 8 * s : 8 * s + 8, :] = jnp.where(first, sums[1], sums[0])


def slot_sums(k, panel, layout, arrays, flops):
    depth, n = panel.shape
    tile = min(n, 256)
    rows = 8 * len(layout)
    out = jax.ShapeDtypeStruct((HI * Z, rows, n), jnp.float32)
    return pl.pallas_call(
        functools.partial(slot_sums_kernel, layout),
        grid=(n // tile,),
        in_specs=[SCALARS, pl.BlockSpec((depth, tile), lambda j: (0, j))]
        + [pl.BlockSpec(a.shape, lambda j: (0, 0)) for a in arrays],
        out_specs=[pl.BlockSpec((HI * Z, rows, tile), lambda j: (0, 0, j))] * 2,
        out_shape=[out, out],
        compiler_params=pltpu.CompilerParams(vmem_limit_bytes=40 * 2**20),
        cost_estimate=pl.CostEstimate(flops=flops, bytes_accessed=0, transcendentals=0),
    )(k.reshape(1), panel, *arrays)


def core_sum(mine, theirs):
    return ((mine + lax.ppermute(theirs, "col", CORE_SWAP)) * SCALE).astype(jnp.float16)


def send_to_slots(parts):
    got = lax.all_to_all(
        parts, "col", split_axis=0, concat_axis=0, axis_index_groups=HZ_GROUPS, tiled=True
    )
    return got.astype(jnp.float32).sum(0)


def send_to_z(parts):
    return lax.all_to_all(
        parts, "col", split_axis=0, concat_axis=0, axis_index_groups=Z_GROUPS, tiled=True
    )


def exact_dot(a, b):
    return jnp.dot(
        a, b, precision=lax.Precision.HIGHEST, preferred_element_type=jnp.float32
    )


def whole(kernel, scalars, arrays, rows, n):
    tile = n

    def block(shape):
        if shape[-1] != n:
            return pl.BlockSpec(shape, lambda j: (0,) * len(shape))
        return pl.BlockSpec(shape[:-1] + (tile,), lambda j: (0,) * (len(shape) - 1) + (j,))

    return pl.pallas_call(
        kernel,
        grid=(n // tile,),
        in_specs=[SCALARS] + [block(a.shape) for a in arrays],
        out_specs=block((rows, n)),
        out_shape=jax.ShapeDtypeStruct((rows, n), jnp.float32),
        compiler_params=pltpu.CompilerParams(vmem_limit_bytes=32 * 2**20),
        cost_estimate=pl.CostEstimate(
            flops=0, bytes_accessed=sum(a.size * a.dtype.itemsize for a in arrays), transcendentals=0
        ),
    )(scalars, *arrays)


def fock_matrix(fock_ref):
    ej, el = grid(128, 128)
    return jnp.where((ej >> 6) == (el >> 6), fock_ref[...], 0.0)


def fock_kernel(_, fock_ref, slab_ref, out_ref):
    out_ref[...] = exact_dot(fock_matrix(fock_ref), slab_ref[...].astype(jnp.float32))


def spread_kernel(at_ref, first_ref, second_ref, fock_ref, out_ref):
    x, l, c = at_ref[0], at_ref[1], slot_of(at_ref[2])
    to, at = grid(256, 64)
    source, rho = at >> 3, at & 7
    i = jnp.zeros_like(at)
    for s, ranges in enumerate(SOURCES):
        options = []
        for (kind, dx, dl), narrow in zip(ranges, (False, True, True)):
            group, half = (x + dx) & 3, l ^ dl
            if kind == OWN:
                options.append((group << 4) + (half << 3) + rho)
            elif narrow:
                opposite = (group + 2) & 3
                options.append((opposite << 4) + ((half ^ (opposite >> 1)) << 3) + ((rho - c) & 7))
            else:
                options.append((((group + 3) & 3) << 4) + (((half << 3) + rho - c) & 15))
        chosen = jnp.where(c < 16, options[0], jnp.where(c < 24, options[1], options[2]))
        i = jnp.where(source == s, chosen, i)
    wanted = ((to >> 3) << 1) + (to & 1)
    held = jnp.where((to & 2) == 0, i, partner_of(i, c))
    spread = jnp.where((wanted == held) & ((to & 4) == 0), LADDER_SCALE / SCALE, 0.0)
    to, ej = grid(256, 128)
    order = ((((to >> 1) & 1) << 6) + ((to >> 3) << 1) + (to & 1) == ej) & ((to & 4) != 0)
    out_ref[...] = exact_dot(
        jnp.concatenate([spread, jnp.where(order, FOCK_SCALE, 0.0)], axis=1),
        jnp.concatenate([first_ref[...], second_ref[...], fock_ref[...]]),
    )


def update_kernel(at_ref, fock_ref, got_ref, out_ref):
    ej, at = grid(128, 256)
    e, j = ej >> 6, ej & 63
    i, peer, mine = 2 * at_ref[2] + e, at >> 3, (at & 1) == e
    t = slot_of(peer)
    weight = jnp.where(t == 31, 1 / LADDER_SCALE, 2 / LADDER_SCALE)
    forward = jnp.where(mine & ((at & 6) == 0) & (partner_of(i, t) == j), weight, 0.0)
    backward = jnp.where(mine & ((at & 6) == 2) & (partner_of(j, t) == i), weight, 0.0)
    mirror = jnp.where(mine & ((at & 4) != 0) & ((peer << 1) + ((at >> 1) & 1) == j), 1 / FOCK_SCALE, 0.0)
    out_ref[...] = fock_ref[...] + exact_dot(forward - backward - mirror, got_ref[...])


def exchange(rows):
    return lax.all_to_all(rows, "col", split_axis=0, concat_axis=0, tiled=True)


def per_device(amplitudes, integrals, cd_irreps, ab_irreps, slab, occ_fock):
    r, c = lax.axis_index("row"), lax.axis_index("col")
    k = c % 2
    place = jnp.stack([r // 2, r % 2, c])
    n = integrals.shape[1]
    fock_twice = jnp.tile(occ_fock.T, (2, 2))

    own, to_right, mirrored = by_depth(
        own_pairs_kernel,
        [r.reshape(1)],
        [amplitudes],
        (256, 256, 192),
        scratch=[pltpu.VMEM((448, 512), jnp.bfloat16)],
    )
    partner = lax.ppermute(own, "row", Y_SWAP)
    right = lax.ppermute(own, "row", x_shift(-1))
    left = lax.ppermute(to_right, "row", x_shift(1))
    fock = whole(fock_kernel, place, [fock_twice, slab], 128, n)
    integrals, _ = lax.optimization_barrier((integrals, own))
    panel = masked_tiles(integrals, cd_irreps, ab_irreps)
    other_panel = lax.ppermute(panel, "col", CORE_SWAP)

    partner, left, right, panel = lax.optimization_barrier((partner, left, right, panel))
    to_right, to_partner, to_far, to_core = by_depth(
        second_phase_kernel,
        [k.reshape(1)],
        [own, partner, right, left, mirrored],
        (192, 320, 64, 512),
    )
    to_right, to_partner, to_far, to_core, partner, left, right, panel = lax.optimization_barrier(
        (to_right, to_partner, to_far, to_core, partner, left, right, panel)
    )
    from_core = lax.ppermute(to_core, "col", CORE_SWAP)
    right_partner = lax.ppermute(partner, "row", x_shift(-1))
    from_left = lax.ppermute(to_right, "row", x_shift(1))
    across = lax.ppermute(to_partner, "row", Y_SWAP)
    far = lax.ppermute(to_far, "row", x_shift(2))

    first = first_sums(k, panel, other_panel, [own, partner, right, left, from_core])
    first = send_to_z((first * SCALE).astype(jnp.float16))
    mine, theirs = slot_sums(
        k, panel, SECOND, [right_partner, mirrored, from_left, across, far], COST
    )
    theirs, first = lax.optimization_barrier((theirs, first))
    first = first.astype(jnp.float32).sum(0).reshape(HI, -1, n)
    h = c // 16
    kept = lax.dynamic_index_in_dim(first, h, 0, keepdims=False)
    other = lax.dynamic_index_in_dim(first, 1 - h, 0, keepdims=False)
    first = kept + lax.ppermute(other, "col", H_SWAP)
    second = send_to_slots(core_sum(mine, theirs))

    sent = whole(spread_kernel, place, [first, second, fock], 256, n).astype(jnp.float16)
    got = exchange(sent).astype(jnp.float32)
    return whole(update_kernel, place, [fock, got], 128, n)


def solution(mesh):
    return jax.shard_map(
        per_device,
        mesh=mesh,
        in_specs=(P("row", "col"), P("col", "row"), P("col"), P("row"), P("col", "row"), P()),
        out_specs=P("col", "row"),
        check_vma=False,
    )
```

```python
import functools

import jax
import jax.numpy as jnp
from jax import lax
from jax.experimental import pallas as pl
from jax.experimental.pallas import tpu as pltpu
from jax.sharding import PartitionSpec as P

X, LO, HI, Z, CORES = 4, 2, 2, 8, 2
COLS = HI * Z * CORES
SCALE = 64.0
LADDER_SCALE, FOCK_SCALE = 4.0, 128.0
COST = 40 * 10**9
SCALARS = pl.BlockSpec(memory_space=pltpu.SMEM)


def x_shift(step):
    return [(2 * x + l, 2 * ((x + step) % X) + l) for x in range(X) for l in range(LO)]


Y_SWAP = [(r, r ^ 1) for r in range(X * LO)]
CORE_SWAP = [(c, c ^ 1) for c in range(COLS)]
H_SWAP = [(c, c ^ 16) for c in range(COLS)]
Z_GROUPS = [[16 * h + 2 * z + k for z in range(Z)] for h in range(HI) for k in range(CORES)]
HZ_GROUPS = [[2 * hz + k for hz in range(HI * Z)] for k in range(CORES)]


def partner_of(i, t):
    group, half = i >> 4, (i >> 3) & 1
    following = (((group + 1) & 3) << 4) + ((i + t) & 15)
    opposite = (((group + 2) & 3) << 4) + ((half ^ (group >> 1)) << 3) + ((i + t) & 7)
    same = (group << 4) + ((i + t - 23) & 15)
    return jnp.where(t < 16, following, jnp.where(t < 24, opposite, same))


def slot_of(c):
    return ((c & 1) << 4) + (c >> 1)


def grid(rows, columns):
    return (
        lax.broadcasted_iota(jnp.int32, (rows, columns), 0),
        lax.broadcasted_iota(jnp.int32, (rows, columns), 1),
    )


def masked_tiles_kernel(cd_ref, ab_ref, integrals_ref, out_ref):
    j = pl.program_id(0)
    row_tiles = cd_ref.shape[0]
    size = integrals_ref.shape[0] // row_tiles
    for b in range(integrals_ref.shape[1] // size):
        irrep = ab_ref[j * (integrals_ref.shape[1] // size) + b]
        for a in range(row_tiles):
            at = (slice(a * size, a * size + size), slice(b * size, b * size + size))
            matching = (cd_ref[a] == irrep).astype(jnp.float32).astype(jnp.bfloat16)
            out_ref[at] = integrals_ref[at] * matching


def masked_tiles(integrals, cd_irreps, ab_irreps):
    depth, n = integrals.shape
    tile = min(n, 256)
    block = pl.BlockSpec((depth, tile), lambda j: (0, j))
    return pl.pallas_call(
        masked_tiles_kernel,
        grid=(n // tile,),
        in_specs=[SCALARS, SCALARS, block],
        out_specs=block,
        out_shape=jax.ShapeDtypeStruct((depth, n), jnp.bfloat16),
        compiler_params=pltpu.CompilerParams(vmem_limit_bytes=16 * 2**20),
        cost_estimate=pl.CostEstimate(flops=0, bytes_accessed=4 * depth * n, transcendentals=0),
    )(cd_irreps, ab_irreps, integrals)


def own_pairs_kernel(r_ref, amplitudes_ref, own_ref, right_ref, mirrored_ref, pick_ref):
    @pl.when(pl.program_id(0) == 0)
    def _():
        r = r_ref[0]
        x, l = r >> 1, r & 1
        to, held = grid(448, 512)
        rho, j = to & 7, (r << 3) + (to & 7)
        t = to >> 3
        direct = (rho << 6) + partner_of(j, t)
        before = (((x + 3) & 3) << 4) + ((j - t) & 15)
        opposite = (x + 2) & 3
        across = (opposite << 4) + ((l ^ (opposite >> 1)) << 3) + ((j - t) & 7)
        wanted = jnp.where(to < 256, direct, (rho << 6) + jnp.where(to < 384, before, across))
        sign = jnp.where(to < 256, 1.0, -1.0)
        pick_ref[...] = jnp.where(wanted == held, sign, 0.0).astype(jnp.bfloat16)

    rows = jnp.dot(pick_ref[...], amplitudes_ref[...], preferred_element_type=jnp.float32)
    rows = rows.astype(jnp.bfloat16)
    own_ref[...] = rows[:256]
    right_ref[...] = rows[128:384]
    mirrored_ref[...] = rows[256:]


def by_depth(kernel, scalars, arrays, out_rows, flops=0, scratch=()):
    depth = arrays[0].shape[1]
    tile = min(depth, 512)
    outs = [jax.ShapeDtypeStruct((rows, depth), jnp.bfloat16) for rows in out_rows]
    return pl.pallas_call(
        kernel,
        grid=(depth // tile,),
        in_specs=[SCALARS] * len(scalars)
        + [pl.BlockSpec((a.shape[0], tile), lambda j: (0, j)) for a in arrays],
        out_specs=[pl.BlockSpec((rows, tile), lambda j: (0, j)) for rows in out_rows],
        out_shape=outs,
        scratch_shapes=scratch,
        compiler_params=pltpu.CompilerParams(vmem_limit_bytes=32 * 2**20),
        cost_estimate=pl.CostEstimate(flops=flops, bytes_accessed=0, transcendentals=0),
    )(*scalars, *arrays)


def second_phase_kernel(
    k_ref, own_ref, partner_ref, right_ref, left_ref, mirrored_ref, right_out, across_out, far_out, core_out
):
    right_out[:128] = partner_ref[128:]
    right_out[128:] = left_ref[64:128]
    across_out[:192] = mirrored_ref[...]
    across_out[192:] = left_ref[128:]
    far_out[...] = partner_ref[192:]
    core_out[...] = core_rows(1 - k_ref[0], own_ref, partner_ref, right_ref, left_ref)


def core_rows(k, own_ref, partner_ref, right_ref, left_ref):
    at, at_left = pl.multiple_of(128 * k, 128), pl.multiple_of(128 * (1 - k), 128)
    return jnp.concatenate(
        [ref[pl.ds(at, 128), :] for ref in (own_ref, partner_ref, right_ref)]
        + [left_ref[pl.ds(at_left, 128), :]]
    )


def first_sums_kernel(
    k_ref, panel_ref, other_panel_ref, own_ref, partner_ref, right_ref, left_ref, got_ref, out_ref
):
    rows = core_rows(k_ref[0], own_ref, partner_ref, right_ref, left_ref)
    sums = jnp.dot(rows, panel_ref[...], preferred_element_type=jnp.float32)
    sums += jnp.dot(got_ref[...], other_panel_ref[...], preferred_element_type=jnp.float32)
    for s in range(4):
        source = sums[128 * s : 128 * s + 128].reshape(HI, Z, 8, sums.shape[1])
        for h in range(HI):
            out_ref[:, 32 * h + 8 * s : 32 * h + 8 * s + 8, :] = source[h]


def first_sums(k, panel, other_panel, arrays):
    depth, n = panel.shape
    tile = min(n, 256)
    column = pl.BlockSpec((depth, tile), lambda j: (0, j))
    return pl.pallas_call(
        first_sums_kernel,
        grid=(n // tile,),
        in_specs=[SCALARS, column, column] + [pl.BlockSpec(a.shape, lambda j: (0, 0)) for a in arrays],
        out_specs=pl.BlockSpec((Z, HI * 32, tile), lambda j: (0, 0, j)),
        out_shape=jax.ShapeDtypeStruct((Z, HI * 32, n), jnp.float32),
        compiler_params=pltpu.CompilerParams(vmem_limit_bytes=48 * 2**20),
        cost_estimate=pl.CostEstimate(flops=COST, bytes_accessed=0, transcendentals=0),
    )(k.reshape(1), panel, other_panel, *arrays)


OWN, MIRROR = 0, 1
SOURCES = (
    ((OWN, 0, 0),) * 3,
    ((OWN, 0, 1),) * 3,
    ((OWN, 1, 0),) * 3,
    ((MIRROR, 3, 0), (OWN, 3, 0), (OWN, 3, 0)),
    ((OWN, 1, 1),) * 3,
    ((MIRROR, 0, 0), (MIRROR, 0, 0), (OWN, 2, 0)),
    ((MIRROR, 0, 1), (MIRROR, 0, 1), (OWN, 2, 1)),
    ((MIRROR, 3, 1), (OWN, 3, 1), (OWN, 3, 1)),
)
SECOND = (
    ((0, 0, 256),),
    ((1, 0, 192), (2, 128, 192)),
    ((3, 0, 192), (4, 0, 64)),
    ((3, 192, 320), (2, 0, 128)),
)


def slot_sums_kernel(layout, k_ref, panel_ref, *refs):
    *arrays, mine_ref, theirs_ref = refs
    columns = panel_ref.shape[1]
    for s, pieces in enumerate(layout):
        rows = [arrays[at][start:end, :] for at, start, end in pieces]
        rows = rows[0] if len(rows) == 1 else jnp.concatenate(rows)
        sums = jnp.dot(rows, panel_ref[...], preferred_element_type=jnp.float32)
        sums = sums.reshape(CORES, HI * Z, 8, columns)
        first = k_ref[0] == 0
        mine_ref[:, 8 * s : 8 * s + 8, :] = jnp.where(first, sums[0], sums[1])
        theirs_ref[:, 8 * s : 8 * s + 8, :] = jnp.where(first, sums[1], sums[0])


def slot_sums(k, panel, layout, arrays, flops):
    depth, n = panel.shape
    tile = min(n, 256)
    rows = 8 * len(layout)
    out = jax.ShapeDtypeStruct((HI * Z, rows, n), jnp.float32)
    return pl.pallas_call(
        functools.partial(slot_sums_kernel, layout),
        grid=(n // tile,),
        in_specs=[SCALARS, pl.BlockSpec((depth, tile), lambda j: (0, j))]
        + [pl.BlockSpec(a.shape, lambda j: (0, 0)) for a in arrays],
        out_specs=[pl.BlockSpec((HI * Z, rows, tile), lambda j: (0, 0, j))] * 2,
        out_shape=[out, out],
        compiler_params=pltpu.CompilerParams(vmem_limit_bytes=40 * 2**20),
        cost_estimate=pl.CostEstimate(flops=flops, bytes_accessed=0, transcendentals=0),
    )(k.reshape(1), panel, *arrays)


def core_sum(mine, theirs):
    return ((mine + lax.ppermute(theirs, "col", CORE_SWAP)) * SCALE).astype(jnp.float16)


def send_to_slots(parts):
    got = lax.all_to_all(
        parts, "col", split_axis=0, concat_axis=0, axis_index_groups=HZ_GROUPS, tiled=True
    )
    return got.astype(jnp.float32).sum(0)


def send_to_z(parts):
    return lax.all_to_all(
        parts, "col", split_axis=0, concat_axis=0, axis_index_groups=Z_GROUPS, tiled=True
    )


def exact_dot(a, b):
    return jnp.dot(
        a, b, precision=lax.Precision.HIGHEST, preferred_element_type=jnp.float32
    )


def whole(kernel, scalars, arrays, rows, n):
    tile = n

    def block(shape):
        if shape[-1] != n:
            return pl.BlockSpec(shape, lambda j: (0,) * len(shape))
        return pl.BlockSpec(shape[:-1] + (tile,), lambda j: (0,) * (len(shape) - 1) + (j,))

    return pl.pallas_call(
        kernel,
        grid=(n // tile,),
        in_specs=[SCALARS] + [block(a.shape) for a in arrays],
        out_specs=block((rows, n)),
        out_shape=jax.ShapeDtypeStruct((rows, n), jnp.float32),
        compiler_params=pltpu.CompilerParams(vmem_limit_bytes=32 * 2**20),
        cost_estimate=pl.CostEstimate(
            flops=0, bytes_accessed=sum(a.size * a.dtype.itemsize for a in arrays), transcendentals=0
        ),
    )(scalars, *arrays)


def fock_matrix(fock_ref):
    ej, el = grid(128, 128)
    return jnp.where((ej >> 6) == (el >> 6), fock_ref[...], 0.0)


def fock_kernel(_, fock_ref, slab_ref, out_ref):
    out_ref[...] = exact_dot(fock_matrix(fock_ref), slab_ref[...].astype(jnp.float32))


def spread_kernel(at_ref, first_ref, second_ref, fock_ref, out_ref):
    x, l, c = at_ref[0], at_ref[1], slot_of(at_ref[2])
    to, at = grid(256, 64)
    source, rho = at >> 3, at & 7
    i = jnp.zeros_like(at)
    for s, ranges in enumerate(SOURCES):
        options = []
        for (kind, dx, dl), narrow in zip(ranges, (False, True, True)):
            group, half = (x + dx) & 3, l ^ dl
            if kind == OWN:
                options.append((group << 4) + (half << 3) + rho)
            elif narrow:
                opposite = (group + 2) & 3
                options.append((opposite << 4) + ((half ^ (opposite >> 1)) << 3) + ((rho - c) & 7))
            else:
                options.append((((group + 3) & 3) << 4) + (((half << 3) + rho - c) & 15))
        chosen = jnp.where(c < 16, options[0], jnp.where(c < 24, options[1], options[2]))
        i = jnp.where(source == s, chosen, i)
    wanted = ((to >> 3) << 1) + (to & 1)
    held = jnp.where((to & 2) == 0, i, partner_of(i, c))
    spread = jnp.where((wanted == held) & ((to & 4) == 0), LADDER_SCALE / SCALE, 0.0)
    to, ej = grid(256, 128)
    order = ((((to >> 1) & 1) << 6) + ((to >> 3) << 1) + (to & 1) == ej) & ((to & 4) != 0)
    out_ref[...] = exact_dot(
        jnp.concatenate([spread, jnp.where(order, FOCK_SCALE, 0.0)], axis=1),
        jnp.concatenate([first_ref[...], second_ref[...], fock_ref[...]]),
    )


def weights_kernel(at_ref, out_ref):
    ej, at = grid(128, 256)
    e, j = ej >> 6, ej & 63
    i, peer, mine = 2 * at_ref[2] + e, at >> 3, (at & 1) == e
    t = slot_of(peer)
    weight = jnp.where(t == 31, 1 / LADDER_SCALE, 2 / LADDER_SCALE)
    forward = jnp.where(mine & ((at & 6) == 0) & (partner_of(i, t) == j), weight, 0.0)
    backward = jnp.where(mine & ((at & 6) == 2) & (partner_of(j, t) == i), weight, 0.0)
    mirror = jnp.where(
        mine & ((at & 4) != 0) & ((peer << 1) + ((at >> 1) & 1) == j), 1 / FOCK_SCALE, 0.0
    )
    out_ref[...] = forward - backward - mirror


def update_kernel(_, fock_ref, weights_ref, got_ref, out_ref):
    out_ref[...] = fock_ref[...] + exact_dot(weights_ref[...], got_ref[...])


def exchange(rows):
    return lax.all_to_all(rows, "col", split_axis=0, concat_axis=0, tiled=True)


def per_device(amplitudes, integrals, cd_irreps, ab_irreps, slab, occ_fock):
    r, c = lax.axis_index("row"), lax.axis_index("col")
    k = c % 2
    place = jnp.stack([r // 2, r % 2, c])
    n = integrals.shape[1]
    fock_twice = jnp.tile(occ_fock.T, (2, 2))

    own, to_right, mirrored = by_depth(
        own_pairs_kernel,
        [r.reshape(1)],
        [amplitudes],
        (256, 256, 192),
        scratch=[pltpu.VMEM((448, 512), jnp.bfloat16)],
    )
    partner = lax.ppermute(own, "row", Y_SWAP)
    right = lax.ppermute(own, "row", x_shift(-1))
    left = lax.ppermute(to_right, "row", x_shift(1))
    fock = whole(fock_kernel, place, [fock_twice, slab], 128, n)
    integrals, _ = lax.optimization_barrier((integrals, own))
    panel = masked_tiles(integrals, cd_irreps, ab_irreps)
    other_panel = lax.ppermute(panel, "col", CORE_SWAP)

    partner, left, right, panel = lax.optimization_barrier((partner, left, right, panel))
    to_right, to_partner, to_far, to_core = by_depth(
        second_phase_kernel,
        [k.reshape(1)],
        [own, partner, right, left, mirrored],
        (192, 320, 64, 512),
    )
    to_right, to_partner, to_far, to_core, partner, left, right, panel = lax.optimization_barrier(
        (to_right, to_partner, to_far, to_core, partner, left, right, panel)
    )
    from_core = lax.ppermute(to_core, "col", CORE_SWAP)
    right_partner = lax.ppermute(partner, "row", x_shift(-1))
    from_left = lax.ppermute(to_right, "row", x_shift(1))
    across = lax.ppermute(to_partner, "row", Y_SWAP)
    far = lax.ppermute(to_far, "row", x_shift(2))

    first = first_sums(k, panel, other_panel, [own, partner, right, left, from_core])
    first = send_to_z((first * SCALE).astype(jnp.float16))
    mine, theirs = slot_sums(
        k, panel, SECOND, [right_partner, mirrored, from_left, across, far], COST
    )
    weights = whole(weights_kernel, place, [], 128, 256)
    theirs, first, weights = lax.optimization_barrier((theirs, first, weights))
    first = first.astype(jnp.float32).sum(0).reshape(HI, -1, n)
    h = c // 16
    kept = lax.dynamic_index_in_dim(first, h, 0, keepdims=False)
    other = lax.dynamic_index_in_dim(first, 1 - h, 0, keepdims=False)
    first = kept + lax.ppermute(other, "col", H_SWAP)
    second = send_to_slots(core_sum(mine, theirs))

    sent = whole(spread_kernel, place, [first, second, fock], 256, n).astype(jnp.float16)
    got = exchange(sent).astype(jnp.float32)
    return whole(update_kernel, place, [fock, weights, got], 128, n)


def solution(mesh):
    return jax.shard_map(
        per_device,
        mesh=mesh,
        in_specs=(P("row", "col"), P("col", "row"), P("col"), P("row"), P("col", "row"), P()),
        out_specs=P("col", "row"),
        check_vma=False,
    )
```
